512 devices in a mesh: row: 8 (over z_hi, core), col: 8 (over z_lo, x), dep: 8 (over y).
Axes of the slice: x: 4, y: 8, z: 8 (z_hi: 4, z_lo: 2; z = z_hi * 2 + z_lo), core: 2. Of those that a mesh axis runs over, the one named last changes fastest.
Arguments:
- inputs: bfloat16 [4096, 6144], P(('row', 'dep'), 'col'), may hold values from -16 to 16
- weight: bfloat16 [6144, 24576], P(('col', 'row'), 'dep'), may hold values from -0.078125 to 0.078125
- grad_out: bfloat16 [4096, 24576], P(('row', 'col'), 'dep'), may hold values from -16 to 16
Outputs:
- hidden: bfloat16 [4096, 24576], P(('row', 'col'), 'dep')
- grad_inputs: bfloat16 [4096, 6144], P(('row', 'dep'), 'col')
The draws below stay inside these ranges and needn't reach their ends.
All inputs are finite; a program needn't handle non-finite values.
Results may differ from the reference program's by a relative error of at most 0.022.
Values may be sent and summed in bfloat16 or wider, within the bound.
A program may use at most 64 MiB of HBM per device.

```python
import jax
import jax.numpy as jnp
from jax import lax

D = 6144
FF = 24576
TOKENS = 4096
N_COL = 8
N_DEP = 8


def strengthened(result, stream_key, source, target, shards_of, factor):
    def block_of(dim):
        return (jnp.arange(result.shape[dim]) // (result.shape[dim] // shards_of)).reshape((-1,) + (1,) * (result.ndim - 1 - dim))

    near = jax.random.permutation(stream_key, shards_of)[block_of(target)]
    second = (block_of(target) + shards_of // 2) % shards_of
    return jnp.where((block_of(source) == near) | (block_of(source) == second), factor * result, result)


def level_of(own_key, dims, cuts, low, largest):
    factor_of = 1.0
    for dim, shards_of in cuts:
        draws = jax.random.uniform(jax.random.fold_in(jax.random.fold_in(own_key, 6), dim), (shards_of,), jnp.float32, low / len(cuts), largest / len(cuts))
        factor_of = factor_of * jnp.repeat(jnp.exp(draws), dims[dim] // shards_of).reshape((-1,) + (1,) * (len(dims) - 1 - dim))
    return factor_of


def centred(rng, dims, spread, bound, split=(), kind=jnp.bfloat16):
    drawn = spread * jax.random.normal(rng, dims, jnp.float32)
    if split:
        drawn = drawn * level_of(rng, dims, split, -0.22, 0.18)
    return jnp.clip(drawn, -bound, bound).astype(kind)


def gaussian_with(key, dims, width, limit, pieces, heavy, kind=jnp.bfloat16):
    array = width * jax.random.normal(key, dims, jnp.float32)
    if pieces:
        array = array * level_of(key, dims, pieces, -0.22, 0.18)
    return jnp.clip(strengthened(array, jax.random.fold_in(key, 3), *heavy), -limit, limit).astype(kind)


def setup_inputs(seed: int = 0) -> dict:
    streams_of = jax.random.split(jax.random.key(seed), 4)
    return {
        "inputs": gaussian_with(streams_of[0], (TOKENS, D), 1.0, 16.0, ((0, 64), (1, 8)), (1, 0, 64, 4.0)),
        "weight": centred(streams_of[1], (D, FF), D ** -0.5, 0.078125, ((0, 64), (1, 8))),
        "grad_out": gaussian_with(streams_of[2], (TOKENS, FF), 1.0, 16.0, ((0, 64), (1, 8)), (1, 0, 64, 4.0)),
    }


def gelu_tanh(values):
    return jax.nn.gelu(values, approximate=True)

def reference(inputs, weight, grad_out):
    width_block = D // N_COL
    hidden_block = FF // N_DEP

    def fwd_term(running, position):
        columns = lax.dynamic_slice_in_dim(inputs, position * width_block, width_block, 1)
        row_block = lax.dynamic_slice_in_dim(weight, position * width_block, width_block, 0)
        product = jnp.dot(columns, row_block, preferred_element_type=jnp.float32).astype(jnp.bfloat16)
        product = lax.optimization_barrier(product).astype(jnp.float32)
        return (running + product, None)
    pre_act, _ = lax.scan(fwd_term, jnp.zeros((TOKENS, FF), jnp.float32), jnp.arange(N_COL, dtype=jnp.int32))
    activation, pullback = jax.vjp(gelu_tanh, pre_act)
    hidden = activation.astype(jnp.bfloat16)
    grad_pre = pullback(grad_out.astype(jnp.float32))[0].astype(jnp.bfloat16)

    def bwd_term(running, position):
        grad_cols = lax.dynamic_slice_in_dim(grad_pre, position * hidden_block, hidden_block, 1)
        weight_cols = lax.dynamic_slice_in_dim(weight, position * hidden_block, hidden_block, 1)
        product = lax.dot_general(grad_cols, weight_cols, (((1,), (1,)), ((), ())), preferred_element_type=jnp.float32).astype(jnp.bfloat16)
        product = lax.optimization_barrier(product).astype(jnp.float32)
        return (running + product, None)
    grad_sum, _ = lax.scan(bwd_term, jnp.zeros((TOKENS, D), jnp.float32), jnp.arange(N_DEP, dtype=jnp.int32))
    return (hidden, grad_sum.astype(jnp.bfloat16))
```

```python
import math

import jax
import jax.numpy as jnp
from jax import lax
from jax.experimental import pallas as pl
from jax.experimental.pallas import tpu as pltpu
from jax.sharding import PartitionSpec as P

MESH = pl.DeviceIdType.MESH
BF16, F32 = jnp.bfloat16, jnp.float32
CHUNK = 256
AHEAD = 1
NZ, NX, NY = 8, 4, 8
FWD, ACT, BWD = 5, 7, 9


def gelu_and_slope(v):
    c0 = math.sqrt(2.0 / math.pi)
    sq = v * v
    t = jnp.tanh(c0 * v * (1.0 + 0.044715 * sq))
    half = 0.5 * (1.0 + t)
    slope = half + 0.5 * v * (1.0 - t * t) * (c0 * (1.0 + 3.0 * 0.044715 * sq))
    return v * half, slope


def kernel(x_ref, w_ref, g_ref, hid_ref, out_ref, wbuf, xbuf, xsend, xrecv, gbuf, acc, ysend, yrecv, jump,
           z_ss, z_rs, sib_ss, sib_rs, own_s, f_ss, f_rs, b_ss, b_rs, h_ss, h_rs, y_ss, y_rs, j_ss, j_rs):
    n = wbuf.shape[0]
    piece, width = xbuf.shape[1], xbuf.shape[2]
    part = w_ref.shape[0]
    cut = part // 2
    row, col, y = lax.axis_index("row"), lax.axis_index("col"), lax.axis_index("dep")
    z_hi, core = row // 2, row % 2
    z_lo, x = col // 4, col % 4
    z = 2 * z_hi + z_lo

    def dev(z_, core_, x_, y_):
        return {"row": (z_ // 2) * 2 + core_, "col": (z_ % 2) * 4 + x_, "dep": y_}

    def slot(z_):
        return (z_ % 2) * 4 + z_ // 2

    up, down = dev((z + 1) % NZ, core, x, y), dev((z + 7) % NZ, core, x, y)
    sibling = dev(z, 1 - core, x, y)
    xs = [dev(z, core, (x + i) % NX, y) for i in range(1, NX)]
    ys = [dev(z, core, x, (y + i) % NY) for i in range(1, NY)]
    far = {"row": row, "col": (1 - z_lo) * 4 + x, "dep": (y + 4) % NY}
    at_home = (y // 4) == z_lo
    mine = slot(z)

    def remote(src, dst, ss, rs, to):
        return pltpu.make_async_remote_copy(src_ref=src, dst_ref=dst, send_sem=ss, recv_sem=rs, device_id=to, device_id_type=MESH)

    def cols(k):
        return pl.ds(pl.multiple_of(k * CHUNK, CHUNK), CHUNK)

    def hop(way, h, k):
        rows = pl.ds(0, part) if h < 4 else pl.ds(way * cut, cut)
        origin = (z - (h - 1) + NZ) % NZ if way == 0 else (z + (h - 1)) % NZ
        to = up if way == 0 else down
        dst = wbuf.at[k, slot(origin), core, rows]
        src = w_ref.at[:, cols(k)] if h == 1 else dst
        return remote(src, dst, z_ss.at[way, h - 1, k], z_rs.at[way, h - 1, k], to)

    def own(k):
        return pltpu.make_async_copy(w_ref.at[:, cols(k)], wbuf.at[k, mine, core], own_s.at[k])

    def to_sibling(k):
        there = wbuf.at[k, :, core]
        return remote(there, there, sib_ss.at[k], sib_rs.at[k], sibling)

    def from_sibling(k):
        there = wbuf.at[k, :, 1 - core]
        return remote(there, there, sib_ss.at[k], sib_rs.at[k], sibling)

    def fwd_copy(i, k):
        return remote(xsend.at[k, (x + i) % NX], xrecv.at[k, i - 1], f_ss.at[i - 1, k], f_rs.at[i - 1, k], xs[i - 1])

    def bwd_copy(i, k):
        return remote(gbuf.at[k, x], gbuf.at[k, x], b_ss.at[i - 1, k], b_rs.at[i - 1, k], xs[i - 1])

    def bwd_arrival(i, k):
        there = gbuf.at[k, (x + NX - i) % NX]
        return remote(there, there, b_ss.at[i - 1, k], b_rs.at[i - 1, k], xs[i - 1])

    def head_copy(i):
        return remote(xbuf.at[y], xbuf.at[y], h_ss.at[i - 1], h_rs.at[i - 1], ys[i - 1])

    def head_arrival(i):
        there = xbuf.at[(y + NY - i) % NY]
        return remote(there, there, h_ss.at[i - 1], h_rs.at[i - 1], ys[i - 1])

    barrier = pltpu.get_barrier_semaphore()
    peers = [up, down, sibling, far] + xs + ys
    for peer in peers:
        pl.semaphore_signal(barrier, inc=1, device_id=peer, device_id_type=MESH)
    pl.semaphore_wait(barrier, len(peers))

    for k in range(AHEAD):
        hop(0, 1, k).start()
        hop(1, 1, k).start()

    swap_in = remote(x_ref, xbuf.at[(y + 4) % NY], j_ss.at[0], j_rs.at[0], far)
    swap_arrival = remote(x_ref, xbuf.at[y], j_ss.at[0], j_rs.at[0], far)
    stay_in = pltpu.make_async_copy(x_ref, xbuf.at[y], j_ss.at[1])

    @pl.when(at_home)
    def _():
        stay_in.start()
        stay_in.wait()

    @pl.when(jnp.logical_not(at_home))
    def _():
        swap_in.start()

    def start_own(k, carry):
        own(k).start()
        return carry

    lax.fori_loop(0, n, start_own, 0)
    acc[...] = jnp.zeros_like(acc)

    @pl.when(jnp.logical_not(at_home))
    def _():
        swap_in.wait_send()
        swap_arrival.wait_recv()

    for i in (4, 3, 5, 2, 6, 1, 7):
        head_copy(i).start()

    def within(k, f):
        pl.when(jnp.logical_and(k >= 0, k < n))(lambda: f(k))

    def pass_on(h):
        def f(k):
            for way in (0, 1):
                hop(way, h, k).wait_recv()
                if h < 4:
                    hop(way, h + 1, k).start()
            if h == 4:
                own(k).wait()
                to_sibling(k).start()
        return f

    def send_own(k):
        hop(0, 1, k).start()
        hop(1, 1, k).start()

    def forward(k):
        @pl.when(k == 0)
        def _():
            for i in range(1, NY):
                head_arrival(i).wait_recv()
        from_sibling(k).wait_recv()
        total = None
        for h in (0, 1):
            a = xbuf[h * 4:(h + 1) * 4].reshape(4 * piece, width)
            w = wbuf[k, h * 4:(h + 1) * 4].reshape(width, CHUNK)
            term = jnp.dot(a, w, preferred_element_type=F32)
            total = term if total is None else total + term
        xsend[k] = total.astype(BF16).reshape(NX, piece, CHUNK)
        for i in (2, 1, 3):
            fwd_copy(i, k).start()

    def activate(k):
        for i in (1, 2, 3):
            fwd_copy(i, k).wait_recv()
        pre = xsend[k, x].astype(F32)
        for i in range(NX - 1):
            pre = pre + xrecv[k, i].astype(F32)
        act, slope = gelu_and_slope(pre)
        hid_ref[:, cols(k)] = act.astype(BF16)
        gbuf[k, x] = (g_ref[:, cols(k)].astype(F32) * slope).astype(BF16)
        for i in (2, 1, 3):
            bwd_copy(i, k).start()

    def backward(k):
        for i in (1, 2, 3):
            bwd_arrival(i, k).wait_recv()
        g = gbuf[k].reshape(4 * piece, CHUNK)
        for h in (0, 1):
            w = wbuf[k, h * 4:(h + 1) * 4].reshape(width, CHUNK)
            acc[h] += lax.dot_general(g, w, (((1,), (1,)), ((), ())), preferred_element_type=F32)

    def one_round(r, carry):
        for h in (4, 3, 2, 1):
            within(r - h, pass_on(h))
        within(r + AHEAD, send_own)
        within(r - FWD, forward)
        within(r - ACT, activate)
        within(r - BWD, backward)
        return carry

    lax.fori_loop(0, n + BWD, one_round, 0)

    half = piece // 2

    def own_rows(p, sub):
        return acc[p // 4, pl.ds(pl.multiple_of((p % 4) * piece + sub * half, half), half)]

    def y_copy(way, h, sub):
        rows = pl.ds(sub * half, half)
        to = ys[0] if way == 0 else ys[NY - 2]
        return remote(ysend.at[way, h - 1, rows], yrecv.at[way, h - 1, rows], y_ss.at[way, h - 1, sub], y_rs.at[way, h - 1, sub], to)

    for h in (1, 2, 3, 4):
        for order in (0, 1):
            for way in (0, 1):
                sub = order if way == 0 else 1 - order
                if h == 1 and order == 1:
                    continue
                p = (y + 5 - h) % NY if way == 0 else (y + h + 3) % NY
                rows = pl.ds(sub * half, half)
                value = own_rows(p, sub)
                if h > 2 or (h == 2 and order == 0):
                    y_copy(way, h - 1, sub).wait_recv()
                    value = value + yrecv[way, h - 2, rows].astype(F32)
                ysend[way, h - 1, rows] = value.astype(BF16)
                y_copy(way, h, sub).start()
    for sub in (0, 1):
        rows = pl.ds(sub * half, half)
        value = own_rows(y, sub)
        for way in (0, 1):
            y_copy(way, 4, sub).wait_recv()
            value = value + yrecv[way, 3, rows].astype(F32)
        jump[rows] = value.astype(BF16)
    swap_out = remote(jump, out_ref, j_ss.at[2], j_rs.at[1], far)

    @pl.when(jnp.logical_not(at_home))
    def _():
        swap_out.start()
        swap_out.wait()

    @pl.when(at_home)
    def _():
        out_ref[...] = jump[...]

    def drain(k, carry):
        for way in (0, 1):
            for h in (1, 2, 3, 4):
                hop(way, h, k).wait_send()
        to_sibling(k).wait_send()
        for i in (1, 2, 3):
            fwd_copy(i, k).wait_send()
            bwd_copy(i, k).wait_send()
        return carry

    lax.fori_loop(0, n, drain, 0)
    for i in range(1, NY):
        head_copy(i).wait_send()
    for way in (0, 1):
        for h in (1, 2, 3, 4):
            for sub in (0, 1):
                if h > 1 or sub == way:
                    y_copy(way, h, sub).wait_send()


def body(inputs, weight, grad_out):
    piece, width = inputs.shape
    part, units = weight.shape
    n = units // CHUNK
    dma = pltpu.SemaphoreType.DMA
    vmem = pl.BlockSpec(memory_space=pltpu.VMEM)
    return pl.pallas_call(
        kernel,
        out_shape=(jax.ShapeDtypeStruct((piece, units), BF16), jax.ShapeDtypeStruct((piece, width), BF16)),
        in_specs=[pl.BlockSpec(memory_space=pl.ANY), pl.BlockSpec(memory_space=pl.ANY), vmem],
        out_specs=(vmem, vmem),
        scratch_shapes=[
            pltpu.VMEM((n, NZ, 2, part, CHUNK), BF16),
            pltpu.VMEM((NY, piece, width), BF16),
            pltpu.VMEM((n, NX, piece, CHUNK), BF16),
            pltpu.VMEM((n, NX - 1, piece, CHUNK), BF16),
            pltpu.VMEM((n, NX, piece, CHUNK), BF16),
            pltpu.VMEM((2, 4 * piece, width), F32),
            pltpu.VMEM((2, 4, piece, width), BF16),
            pltpu.VMEM((2, 4, piece, width), BF16),
            pltpu.VMEM((piece, width), BF16),
            dma((2, 4, n)), dma((2, 4, n)), dma((n,)), dma((n,)), dma((n,)),
            dma((3, n)), dma((3, n)), dma((3, n)), dma((3, n)),
            dma((NY - 1,)), dma((NY - 1,)), dma((2, 4, 2)), dma((2, 4, 2)), dma((3,)), dma((2,)),
        ],
        compiler_params=pltpu.CompilerParams(collective_id=0, has_side_effects=True, vmem_limit_bytes=48 << 20),
        name="up_projection",
    )(inputs, weight, grad_out)


def solution(mesh):
    return jax.shard_map(
        body,
        mesh=mesh,
        in_specs=(P(("row", "dep"), "col"), P(("col", "row"), "dep"), P(("row", "col"), "dep")),
        out_specs=(P(("row", "col"), "dep"), P(("row", "dep"), "col")),
        check_vma=False,
    )
```

```python
import math

import jax
import jax.numpy as jnp
from jax import lax
from jax.experimental import pallas as pl
from jax.experimental.pallas import tpu as pltpu
from jax.sharding import PartitionSpec as P

MESH = pl.DeviceIdType.MESH
BF16, F32 = jnp.bfloat16, jnp.float32
CHUNK = 256
HOPS = (1, 3, 5, 7)
ORDER = (4, 3, 2, 1)
AHEAD = 2
NZ, NX, NY = 8, 4, 8
FWD, ACT, BWD = 8, 10, 12
SWAP, SPREAD = 2, 6
HELD = 1


def gelu_and_slope(v):
    c0 = math.sqrt(2.0 / math.pi)
    sq = v * v
    t = jnp.tanh(c0 * v * (1.0 + 0.044715 * sq))
    half = 0.5 * (1.0 + t)
    slope = half + 0.5 * v * (1.0 - t * t) * (c0 * (1.0 + 3.0 * 0.044715 * sq))
    return v * half, slope


def kernel(x_ref, w_ref, g_ref, hid_ref, out_ref, wbuf, xbuf, xsend, xrecv, gbuf, acc, ysend, yrecv, yrelay, total, gout,
           z_ss, z_rs, sib_ss, sib_rs, own_s, f_ss, f_rs, b_ss, b_rs, h_ss, h_rs, y_ss, y_rs, r_ss, r_rs, j_ss, j_rs, g_s, last_ss, last_rs):
    n = wbuf.shape[0]
    piece, width = xbuf.shape[1], xbuf.shape[2]
    part = w_ref.shape[0]
    cut = part // 2
    row, col, y = lax.axis_index("row"), lax.axis_index("col"), lax.axis_index("dep")
    z_hi, core = row // 2, row % 2
    z_lo, x = col // 4, col % 4
    z = 2 * z_hi + z_lo

    def dev(z_, core_, x_, y_):
        return {"row": (z_ // 2) * 2 + core_, "col": (z_ % 2) * 4 + x_, "dep": y_}

    def slot(z_):
        return (z_ % 2) * 4 + z_ // 2

    up, down = dev((z + 1) % NZ, core, x, y), dev((z + 7) % NZ, core, x, y)
    up_other, down_other = dev((z + 1) % NZ, 1 - core, x, y), dev((z + 7) % NZ, 1 - core, x, y)
    sibling = dev(z, 1 - core, x, y)
    xs = [dev(z, core, (x + i) % NX, y) for i in range(1, NX)]
    ys = {i: dev(z, core, x, (y + i + NY) % NY) for i in (1, -1, 2, -2)}
    far = {"row": row, "col": (1 - z_lo) * 4 + x, "dep": (y + 4) % NY}
    at_home = (y // 4) == z_lo

    def flipped(i):
        return {"row": row, "col": (1 - z_lo) * 4 + x, "dep": (y + i + NY) % NY}

    mine = slot(z)

    def remote(src, dst, ss, rs, to):
        return pltpu.make_async_remote_copy(src_ref=src, dst_ref=dst, send_sem=ss, recv_sem=rs, device_id=to, device_id_type=MESH)

    def cols(k):
        return pl.ds(pl.multiple_of(k * CHUNK, CHUNK), CHUNK)

    def hop(way, h, k):
        rows = pl.ds(0, part) if h < 4 else pl.ds(way * cut, cut)
        origin = (z - (h - 1) + NZ) % NZ if way == 0 else (z + (h - 1)) % NZ
        to = up if way == 0 else down
        dst = wbuf.at[k, slot(origin), core, rows]
        src = w_ref.at[:, cols(k)] if h == 1 else dst
        return remote(src, dst, z_ss.at[way, h - 1, k], z_rs.at[way, h - 1, k], to)

    def own(k):
        return pltpu.make_async_copy(w_ref.at[:, cols(k)], wbuf.at[k, mine, core], own_s.at[k])

    def to_sibling(k):
        there = wbuf.at[k, :, core]
        return remote(there, there, sib_ss.at[k], sib_rs.at[k], sibling)

    def from_sibling(k):
        there = wbuf.at[k, :, 1 - core]
        return remote(there, there, sib_ss.at[k], sib_rs.at[k], sibling)

    def one_to_sibling(away):
        there = wbuf.at[n - 1, slot((z + away + NZ) % NZ), core]
        return remote(there, there, last_ss.at[away + 3], last_rs.at[away + 3], sibling)

    def one_from_sibling(away):
        there = wbuf.at[n - 1, slot((z + away + NZ) % NZ), 1 - core]
        return remote(there, there, last_ss.at[away + 3], last_rs.at[away + 3], sibling)

    def last_hop(way):
        origin = (z + (5, 3)[way]) % NZ
        there = wbuf.at[n - 1, slot(origin), core, pl.ds(way * cut, cut)]
        return remote(there, there, last_ss.at[7 + way], last_rs.at[7 + way], (up_other, down_other)[way])

    def last_hop_arrival(way):
        there = wbuf.at[n - 1, slot((z + 4) % NZ), 1 - core, pl.ds(way * cut, cut)]
        return remote(there, there, last_ss.at[7 + way], last_rs.at[7 + way], (up_other, down_other)[way])

    x_half = piece // 2
    halves = (pl.ds(0, x_half), pl.ds(x_half, x_half))

    def fwd_copy(i, k):
        return remote(xsend.at[k, (x + i) % NX], xrecv.at[k, i - 1], f_ss.at[i - 1, k], f_rs.at[i - 1, k], xs[i - 1])

    def bwd_copy(i, k):
        return remote(gbuf.at[k, x], gbuf.at[k, x], b_ss.at[i - 1, k], b_rs.at[i - 1, k], xs[i - 1])

    def bwd_arrival(i, k):
        there = gbuf.at[k, (x + NX - i) % NX]
        return remote(there, there, b_ss.at[i - 1, k], b_rs.at[i - 1, k], xs[i - 1])

    def head_near(i, step, src):
        return remote(src, xbuf.at[y], h_ss.at[i], h_rs.at[i], ys[step])

    def head_near_arrival(i, step):
        there = xbuf.at[(y - step + NY) % NY]
        return remote(there, there, h_ss.at[i], h_rs.at[i], ys[step])

    NEAR = ((0, 2), (1, -2), (2, 1), (3, -1))

    def head_on(i, step, rows, origin):
        there = xbuf.at[(y + origin + NY) % NY, rows]
        return remote(there, there, h_ss.at[i], h_rs.at[i], ys[step])

    whole = pl.ds(0, piece)
    ON = ((4, 2, halves[0], -2), (5, -2, halves[1], 2), (6, 1, whole, -2), (7, -1, whole, 2))

    def head_on_arrival(i, step, rows, origin):
        there = xbuf.at[(y + origin - step + NY) % NY, rows]
        return remote(there, there, h_ss.at[i], h_rs.at[i], ys[step])

    barrier = pltpu.get_barrier_semaphore()
    same = [up, down, far] + xs + list(ys.values()) + [flipped(i) for i in (1, -1, 2, -2)]
    across = [sibling, up_other, down_other]
    for peer in same:
        pl.semaphore_signal(barrier, inc=1, device_id=peer, device_id_type=MESH)

    @pl.when(core == 0)
    def _():
        pl.semaphore_wait(barrier, len(same))

    @pl.when(core == 1)
    def _():
        pl.semaphore_wait(barrier, len(same) + len(across))

    for peer in across:
        pl.semaphore_signal(barrier, inc=1, device_id=peer, device_id_type=MESH)

    for k in range(AHEAD):
        hop(0, 1, k).start()
        hop(1, 1, k).start()

    swap_in = remote(x_ref, xbuf.at[(y + 4) % NY], j_ss.at[0], j_rs.at[0], far)
    swap_arrival = remote(x_ref, xbuf.at[y], j_ss.at[0], j_rs.at[0], far)
    stay_in = pltpu.make_async_copy(x_ref, xbuf.at[y], j_ss.at[1])

    @pl.when(at_home)
    def _():
        for i, step in NEAR:
            head_near(i, step, x_ref).start()
        stay_in.start()

    @pl.when(jnp.logical_not(at_home))
    def _():
        swap_in.start()

    def start_own(k, carry):
        own(k).start()
        return carry

    lax.fori_loop(0, n, start_own, 0)
    load_g = pltpu.make_async_copy(g_ref, gout, g_s)
    load_g.start()
    acc[...] = jnp.zeros_like(acc)

    def swapped():
        @pl.when(jnp.logical_not(at_home))
        def _():
            swap_arrival.wait_recv()
            for i, step in NEAR:
                head_near(i, step, xbuf.at[y]).start()

    def spread():
        for i, step in NEAR[:2]:
            head_near_arrival(i, step).wait_recv()
        for way in ON:
            head_on(*way).start()

    def within(k, f):
        pl.when(jnp.logical_and(k >= 0, k < n))(lambda: f(k))

    def pass_on(h):
        def f(k):
            for way in (0, 1):
                hop(way, h, k).wait_recv()
                if h < 4:
                    hop(way, h + 1, k).start()
                if h == 3:
                    pl.when(k == n - 1)(last_hop(way).start)
                if h < 4:
                    pl.when(k == n - 1)(one_to_sibling(h if way else -h).start)
            if h == 1:
                own(k).wait()
                pl.when(k == n - 1)(one_to_sibling(0).start)
            if h == 4:
                @pl.when(jnp.logical_and(core == 0, k == 0))
                def _():
                    pl.semaphore_wait(barrier, len(across))

                pl.when(k < n - 1)(to_sibling(k).start)
        return f

    def send_own(k):
        hop(0, 1, k).start()
        hop(1, 1, k).start()

    def forward(k):
        @pl.when(k == 0)
        def _():
            pl.when(at_home)(stay_in.wait)
            for i, step in NEAR[2:]:
                head_near_arrival(i, step).wait_recv()
            for way in ON:
                head_on_arrival(*way).wait_recv()
        pl.when(k < n - 1)(from_sibling(k).wait_recv)

        @pl.when(k == n - 1)
        def _():
            for away in range(-3, 4):
                one_from_sibling(away).wait_recv()
            for way in (0, 1):
                last_hop_arrival(way).wait_recv()

        partial = None
        for h in (0, 1):
            a = xbuf[h * 4:(h + 1) * 4].reshape(4 * piece, width)
            w = wbuf[k, h * 4:(h + 1) * 4].reshape(width, CHUNK)
            term = jnp.dot(a, w, preferred_element_type=F32)
            partial = term if partial is None else partial + term
        xsend[k] = partial.astype(BF16).reshape(NX, piece, CHUNK)

        for i in (2, 1, 3):
            fwd_copy(i, k).start()

    def activate(k):
        pl.when(k == 0)(load_g.wait)
        pre = xsend[k, x].astype(F32)
        for i in (1, 2, 3):
            fwd_copy(i, k).wait_recv()
            pre = pre + xrecv[k, i - 1].astype(F32)
        act, slope = gelu_and_slope(pre)
        gbuf[k, x] = (gout[:, cols(k)].astype(F32) * slope).astype(BF16)
        for i in (2, 1, 3):
            bwd_copy(i, k).start()
        hid_ref[:, cols(k)] = act.astype(BF16)

    def backward(k):
        for i in (1, 2, 3):
            bwd_arrival(i, k).wait_recv()
        g = gbuf[k].reshape(4 * piece, CHUNK)
        for h in (0, 1):
            w = wbuf[k, h * 4:(h + 1) * 4].reshape(width, CHUNK)
            acc[h] += lax.dot_general(g, w, (((1,), (1,)), ((), ())), preferred_element_type=F32)

    def stage(r, lag, f):
        @pl.when(r == lag + HELD)
        def _():
            lax.fori_loop(0, HELD, lambda k, carry: (f(k), carry)[1], 0)

        @pl.when(jnp.logical_and(r >= lag + HELD, r < lag + n))
        def _():
            f(r - lag)

    def one_round(r, carry):
        for h in ORDER:
            within(r - HOPS[h - 1], pass_on(h))
        within(r + AHEAD, send_own)
        pl.when(r == SWAP)(swapped)
        pl.when(r == SPREAD)(spread)
        stage(r, FWD, forward)
        stage(r, ACT, activate)
        stage(r, BWD, backward)
        return carry

    lax.fori_loop(0, n + BWD, one_round, 0)

    for h in (0, 1):
        for p in range(4):
            ysend[h * 4 + p] = acc[h, p * piece:(p + 1) * piece].astype(BF16)

    def ring(step, flip):
        return {"row": row, "col": (1 - z_lo if flip else z_lo) * 4 + x, "dep": (y + step + NY) % NY}

    def held(away, flip):
        return ((1 - z_lo if flip else z_lo) * 4 + (y + away + NY) % 4)

    def here(away):
        return ((y + away + NY) % NY) // 4 == z_lo

    first, second = (halves[1], halves[0]), (halves[0], halves[1])
    TO_RELAY = ((-3, -1, first[0], 3, 3), (3, 1, first[1], 4, 4), (-2, 0, whole, 7, 7), (2, 0, whole, 8, 8),
                (-3, -1, second[0], 3, 9), (3, 1, second[1], 4, 10), (-4, -2, second[0], 5, 5), (4, 2, second[1], 6, 6))
    TO_TARGET = ((-1, -1, whole, 0, 0), (1, 1, whole, 1, 1), (0, 0, whole, 2, 2))

    def term(away, step, rows, at, sem, flip):
        return remote(ysend.at[held(away, flip), rows], yrecv.at[at, rows], y_ss.at[sem, flip], y_rs.at[sem], ring(step, flip))

    def each_term(terms, act):
        for t in terms:
            for flip in (0, 1):
                if t[1] or flip:
                    pl.when(here(t[0]))(lambda t=t, flip=flip: act(term(*t, flip)))

    each_term(TO_RELAY, lambda copy: copy.start())

    def arrived(at, rows, sem):
        there = yrecv.at[at, rows]
        remote(there, there, y_ss.at[sem, 0], y_rs.at[sem], ring(1, 0)).wait_recv()
        return yrecv[at, rows].astype(F32)

    def relayed(way, rows, sem):
        return remote(yrelay.at[way, rows], yrecv.at[9 + way, rows], r_ss.at[way, sem], r_rs.at[way, sem], ring((-2, 2)[way], 0))

    for way in (0, 1):
        away = (-2, 2)[way]

        @pl.when(here(away))
        def _():
            yrelay[way] = ysend[held(away, 0)]

        @pl.when(jnp.logical_not(here(away)))
        def _():
            yrelay[way] = arrived(7 + way, whole, 7 + way).astype(BF16)

        there = yrelay.at[way, first[way]]
        there[...] = (there[...].astype(F32) + arrived(3 + way, first[way], 3 + way)).astype(BF16)
        relayed(way, first[way], 0).start()

    each_term(TO_TARGET, lambda copy: copy.start())

    for way in (0, 1):
        there = yrelay.at[way, second[way]]
        there[...] = (there[...].astype(F32) + arrived(3 + way, second[way], 9 + way) + arrived(5 + way, second[way], 5 + way)).astype(BF16)
        relayed(way, second[way], 1).start()

    @pl.when(at_home)
    def _():
        total[...] = ysend[held(0, 0)].astype(F32)

    @pl.when(jnp.logical_not(at_home))
    def _():
        total[...] = arrived(2, whole, 2)

    total[...] += arrived(0, whole, 0) + arrived(1, whole, 1)
    for sem, rows in ((0, first), (1, second)):
        for way in (0, 1):
            relayed(way, rows[way], sem).wait_recv()
            total[rows[way]] += yrecv[9 + way, rows[way]].astype(F32)
    out_ref[...] = total[...].astype(BF16)

    def drain(k, carry):
        for way in (0, 1):
            for h in (1, 2, 3, 4):
                hop(way, h, k).wait_send()
        pl.when(k < n - 1)(to_sibling(k).wait_send)
        for i in (1, 2, 3):
            fwd_copy(i, k).wait_send()
            bwd_copy(i, k).wait_send()
        return carry

    lax.fori_loop(0, n, drain, 0)
    for away in range(-3, 4):
        one_to_sibling(away).wait_send()
    for way in (0, 1):
        last_hop(way).wait_send()
    pl.when(jnp.logical_not(at_home))(swap_in.wait_send)
    for i, step in NEAR:
        head_near(i, step, x_ref).wait_send()
    for way in ON:
        head_on(*way).wait_send()
    each_term(TO_RELAY + TO_TARGET, lambda copy: copy.wait_send())
    for way in (0, 1):
        relayed(way, first[way], 0).wait_send()
        relayed(way, second[way], 1).wait_send()


def body(inputs, weight, grad_out):
    piece, width = inputs.shape
    part, units = weight.shape
    n = units // CHUNK
    dma = pltpu.SemaphoreType.DMA
    vmem = pl.BlockSpec(memory_space=pltpu.VMEM)
    return pl.pallas_call(
        kernel,
        out_shape=(jax.ShapeDtypeStruct((piece, units), BF16), jax.ShapeDtypeStruct((piece, width), BF16)),
        in_specs=[pl.BlockSpec(memory_space=pl.ANY)] * 3,
        out_specs=(vmem, vmem),
        scratch_shapes=[
            pltpu.VMEM((n, NZ, 2, part, CHUNK), BF16),
            pltpu.VMEM((NY, piece, width), BF16),
            pltpu.VMEM((n, NX, piece, CHUNK), BF16),
            pltpu.VMEM((n, NX - 1, piece, CHUNK), BF16),
            pltpu.VMEM((n, NX, piece, CHUNK), BF16),
            pltpu.VMEM((2, 4 * piece, width), F32),
            pltpu.VMEM((8, piece, width), BF16),
            pltpu.VMEM((11, piece, width), BF16),
            pltpu.VMEM((2, piece, width), BF16),
            pltpu.VMEM((piece, width), F32),
            pltpu.VMEM((piece, units), BF16),
            dma((2, 4, n)), dma((2, 4, n)), dma((n,)), dma((n,)), dma((n,)),
            dma((3, n)), dma((3, n)), dma((3, n)), dma((3, n)),
            dma((8,)), dma((8,)), dma((11, 2)), dma((11,)), dma((2, 2)), dma((2, 2)), dma((2,)), dma((1,)), dma, dma((9,)), dma((9,)),
        ],
        compiler_params=pltpu.CompilerParams(collective_id=0, has_side_effects=True, vmem_limit_bytes=60 << 20),
        name="up_projection",
    )(inputs, weight, grad_out)


def solution(mesh):
    return jax.shard_map(
        body,
        mesh=mesh,
        in_specs=(P(("row", "dep"), "col"), P(("col", "row"), "dep"), P(("row", "col"), "dep")),
        out_specs=(P(("row", "col"), "dep"), P(("row", "dep"), "col")),
        check_vma=False,
    )
```

```python
import math

import jax
import jax.numpy as jnp
from jax import lax
from jax.experimental import pallas as pl
from jax.experimental.pallas import tpu as pltpu
from jax.sharding import PartitionSpec as P

MESH = pl.DeviceIdType.MESH
BF16, F32 = jnp.bfloat16, jnp.float32
CHUNK = 256
HOPS = (1, 3, 5, 7)
ORDER = (4, 3, 2, 1)
AHEAD = 2
NZ, NX, NY = 8, 4, 8
VMEM = 55783424
FWD, ACT, BWD = 8, 10, 12
SWAP, SPREAD = 2, 6
HELD = 1


def gelu_and_slope(v):
    c0 = math.sqrt(2.0 / math.pi)
    sq = v * v
    t = jnp.tanh(c0 * v * (1.0 + 0.044715 * sq))
    half = 0.5 * (1.0 + t)
    slope = half + 0.5 * v * (1.0 - t * t) * (c0 * (1.0 + 3.0 * 0.044715 * sq))
    return v * half, slope


def kernel(x_ref, w_ref, g_ref, hid_ref, out_ref, wbuf, xbuf, xsend, xrecv, gbuf, acc, ysend, yrecv, yrelay, total, gout,
           z_ss, z_rs, sib_ss, sib_rs, own_s, f_ss, f_rs, b_ss, b_rs, h_ss, h_rs, y_ss, y_rs, r_ss, r_rs, j_ss, j_rs, g_s, last_ss, last_rs):
    n = wbuf.shape[0]
    piece, width = xbuf.shape[1], xbuf.shape[2]
    part = w_ref.shape[0]
    cut = part // 2
    row, col, y = lax.axis_index("row"), lax.axis_index("col"), lax.axis_index("dep")
    z_hi, core = row // 2, row % 2
    z_lo, x = col // 4, col % 4
    z = 2 * z_hi + z_lo

    def dev(z_, core_, x_, y_):
        return {"row": (z_ // 2) * 2 + core_, "col": (z_ % 2) * 4 + x_, "dep": y_}

    def slot(z_):
        return (z_ % 2) * 4 + z_ // 2

    up, down = dev((z + 1) % NZ, core, x, y), dev((z + 7) % NZ, core, x, y)
    up_other, down_other = dev((z + 1) % NZ, 1 - core, x, y), dev((z + 7) % NZ, 1 - core, x, y)
    sibling = dev(z, 1 - core, x, y)
    xs = [dev(z, core, (x + i) % NX, y) for i in range(1, NX)]
    ys = {i: dev(z, core, x, (y + i + NY) % NY) for i in (1, -1, 2, -2)}
    far = {"row": row, "col": (1 - z_lo) * 4 + x, "dep": (y + 4) % NY}
    at_home = (y // 4) == z_lo

    def flipped(i):
        return {"row": row, "col": (1 - z_lo) * 4 + x, "dep": (y + i + NY) % NY}

    mine = slot(z)

    def remote(src, dst, ss, rs, to):
        return pltpu.make_async_remote_copy(src_ref=src, dst_ref=dst, send_sem=ss, recv_sem=rs, device_id=to, device_id_type=MESH)

    def cols(k):
        return pl.ds(pl.multiple_of(k * CHUNK, CHUNK), CHUNK)

    def hop(way, h, k):
        rows = pl.ds(0, part) if h < 4 else pl.ds(way * cut, cut)
        origin = (z - (h - 1) + NZ) % NZ if way == 0 else (z + (h - 1)) % NZ
        to = up if way == 0 else down
        dst = wbuf.at[k, slot(origin), core, rows]
        src = w_ref.at[:, cols(k)] if h == 1 else dst
        return remote(src, dst, z_ss.at[way, h - 1, k], z_rs.at[way, h - 1, k], to)

    def own(k):
        return pltpu.make_async_copy(w_ref.at[:, cols(k)], wbuf.at[k, mine, core], own_s.at[k])

    def to_sibling(k):
        there = wbuf.at[k, :, core]
        return remote(there, there, sib_ss.at[k], sib_rs.at[k], sibling)

    def from_sibling(k):
        there = wbuf.at[k, :, 1 - core]
        return remote(there, there, sib_ss.at[k], sib_rs.at[k], sibling)

    def one_to_sibling(away):
        there = wbuf.at[n - 1, slot((z + away + NZ) % NZ), core]
        return remote(there, there, last_ss.at[away + 3], last_rs.at[away + 3], sibling)

    def one_from_sibling(away):
        there = wbuf.at[n - 1, slot((z + away + NZ) % NZ), 1 - core]
        return remote(there, there, last_ss.at[away + 3], last_rs.at[away + 3], sibling)

    def last_hop(way):
        origin = (z + (5, 3)[way]) % NZ
        there = wbuf.at[n - 1, slot(origin), core, pl.ds(way * cut, cut)]
        return remote(there, there, last_ss.at[7 + way], last_rs.at[7 + way], (up_other, down_other)[way])

    def last_hop_arrival(way):
        there = wbuf.at[n - 1, slot((z + 4) % NZ), 1 - core, pl.ds(way * cut, cut)]
        return remote(there, there, last_ss.at[7 + way], last_rs.at[7 + way], (up_other, down_other)[way])

    x_half = piece // 2
    halves = (pl.ds(0, x_half), pl.ds(x_half, x_half))

    def fwd_copy(i, k):
        return remote(xsend.at[k, (x + i) % NX], xrecv.at[k, i - 1], f_ss.at[i - 1, k], f_rs.at[i - 1, k], xs[i - 1])

    def bwd_copy(i, k):
        return remote(gbuf.at[k, x], gbuf.at[k, x], b_ss.at[i - 1, k], b_rs.at[i - 1, k], xs[i - 1])

    def bwd_arrival(i, k):
        there = gbuf.at[k, (x + NX - i) % NX]
        return remote(there, there, b_ss.at[i - 1, k], b_rs.at[i - 1, k], xs[i - 1])

    def head_near(i, step, src):
        return remote(src, xbuf.at[y], h_ss.at[i], h_rs.at[i], ys[step])

    def head_near_arrival(i, step):
        there = xbuf.at[(y - step + NY) % NY]
        return remote(there, there, h_ss.at[i], h_rs.at[i], ys[step])

    NEAR = ((0, 2), (1, -2), (2, 1), (3, -1))

    def head_on(i, step, rows, origin):
        there = xbuf.at[(y + origin + NY) % NY, rows]
        return remote(there, there, h_ss.at[i], h_rs.at[i], ys[step])

    whole = pl.ds(0, piece)
    ON = ((4, 2, halves[0], -2), (5, -2, halves[1], 2), (6, 1, whole, -2), (7, -1, whole, 2))

    def head_on_arrival(i, step, rows, origin):
        there = xbuf.at[(y + origin - step + NY) % NY, rows]
        return remote(there, there, h_ss.at[i], h_rs.at[i], ys[step])

    barrier = pltpu.get_barrier_semaphore()
    same = [up, down, far] + xs + list(ys.values()) + [flipped(i) for i in (1, -1, 2, -2)]
    across = [sibling, up_other, down_other]
    for peer in same:
        pl.semaphore_signal(barrier, inc=1, device_id=peer, device_id_type=MESH)

    @pl.when(core == 0)
    def _():
        pl.semaphore_wait(barrier, len(same))

    @pl.when(core == 1)
    def _():
        pl.semaphore_wait(barrier, len(same) + len(across))

    for peer in across:
        pl.semaphore_signal(barrier, inc=1, device_id=peer, device_id_type=MESH)

    for k in range(AHEAD):
        hop(0, 1, k).start()
        hop(1, 1, k).start()

    swap_in = remote(x_ref, xbuf.at[(y + 4) % NY], j_ss.at[0], j_rs.at[0], far)
    swap_arrival = remote(x_ref, xbuf.at[y], j_ss.at[0], j_rs.at[0], far)
    stay_in = pltpu.make_async_copy(x_ref, xbuf.at[y], j_ss.at[1])

    @pl.when(at_home)
    def _():
        for i, step in NEAR:
            head_near(i, step, x_ref).start()
        stay_in.start()

    @pl.when(jnp.logical_not(at_home))
    def _():
        swap_in.start()

    def start_own(k, carry):
        own(k).start()
        return carry

    lax.fori_loop(0, n, start_own, 0)
    load_g = pltpu.make_async_copy(g_ref, gout, g_s)
    load_g.start()
    acc[...] = jnp.zeros_like(acc)

    def swapped():
        @pl.when(jnp.logical_not(at_home))
        def _():
            swap_arrival.wait_recv()
            for i, step in NEAR:
                head_near(i, step, xbuf.at[y]).start()

    def spread():
        for i, step in NEAR[:2]:
            head_near_arrival(i, step).wait_recv()
        for way in ON:
            head_on(*way).start()

    def within(k, f):
        pl.when(jnp.logical_and(k >= 0, k < n))(lambda: f(k))

    def pass_on(h):
        def f(k):
            for way in (0, 1):
                hop(way, h, k).wait_recv()
                if h < 4:
                    hop(way, h + 1, k).start()
                if h == 3:
                    pl.when(k == n - 1)(last_hop(way).start)
                if h < 4:
                    pl.when(k == n - 1)(one_to_sibling(h if way else -h).start)
            if h == 1:
                own(k).wait()
                pl.when(k == n - 1)(one_to_sibling(0).start)
            if h == 4:
                @pl.when(jnp.logical_and(core == 0, k == 0))
                def _():
                    pl.semaphore_wait(barrier, len(across))

                pl.when(k < n - 1)(to_sibling(k).start)
        return f

    def send_own(k):
        hop(0, 1, k).start()
        hop(1, 1, k).start()

    def forward(k):
        @pl.when(k == 0)
        def _():
            pl.when(at_home)(stay_in.wait)
            for i, step in NEAR[2:]:
                head_near_arrival(i, step).wait_recv()
            for way in ON:
                head_on_arrival(*way).wait_recv()
        pl.when(k < n - 1)(from_sibling(k).wait_recv)

        @pl.when(k == n - 1)
        def _():
            for away in range(-3, 4):
                one_from_sibling(away).wait_recv()
            for way in (0, 1):
                last_hop_arrival(way).wait_recv()

        partial = None
        for h in (0, 1):
            a = xbuf[h * 4:(h + 1) * 4].reshape(4 * piece, width)
            w = wbuf[k, h * 4:(h + 1) * 4].reshape(width, CHUNK)
            term = jnp.dot(a, w, preferred_element_type=F32)
            partial = term if partial is None else partial + term
        xsend[k] = partial.astype(BF16).reshape(NX, piece, CHUNK)

        for i in (2, 1, 3):
            fwd_copy(i, k).start()

    def activate(k):
        pl.when(k == 0)(load_g.wait)
        pre = xsend[k, x].astype(F32)
        for i in (1, 2, 3):
            fwd_copy(i, k).wait_recv()
            pre = pre + xrecv[k, i - 1].astype(F32)
        act, slope = gelu_and_slope(pre)
        gbuf[k, x] = (gout[:, cols(k)].astype(F32) * slope).astype(BF16)
        for i in (2, 1, 3):
            bwd_copy(i, k).start()
        hid_ref[:, cols(k)] = act.astype(BF16)

    def backward(k):
        for i in (1, 2, 3):
            bwd_arrival(i, k).wait_recv()
        g = gbuf[k].reshape(4 * piece, CHUNK)
        for h in (0, 1):
            w = wbuf[k, h * 4:(h + 1) * 4].reshape(width, CHUNK)
            acc[h] += lax.dot_general(g, w, (((1,), (1,)), ((), ())), preferred_element_type=F32)

    def stage(r, lag, f):
        @pl.when(r == lag + HELD)
        def _():
            lax.fori_loop(0, HELD, lambda k, carry: (f(k), carry)[1], 0)

        @pl.when(jnp.logical_and(r >= lag + HELD, r < lag + n))
        def _():
            f(r - lag)

    def one_round(r, carry):
        for h in ORDER:
            within(r - HOPS[h - 1], pass_on(h))
        within(r + AHEAD, send_own)
        pl.when(r == SWAP)(swapped)
        pl.when(r == SPREAD)(spread)
        stage(r, FWD, forward)
        stage(r, ACT, activate)
        stage(r, BWD, backward)
        return carry

    lax.fori_loop(0, n + BWD, one_round, 0)

    for h in (0, 1):
        for p in range(4):
            ysend[h * 4 + p] = acc[h, p * piece:(p + 1) * piece].astype(BF16)

    def ring(step, flip):
        return {"row": row, "col": (1 - z_lo if flip else z_lo) * 4 + x, "dep": (y + step + NY) % NY}

    def held(away, flip):
        return ((1 - z_lo if flip else z_lo) * 4 + (y + away + NY) % 4)

    def here(away):
        return ((y + away + NY) % NY) // 4 == z_lo

    first, second = (halves[1], halves[0]), (halves[0], halves[1])
    TO_RELAY = ((-3, -1, first[0], 3, 3), (3, 1, first[1], 4, 4), (-2, 0, whole, 7, 7), (2, 0, whole, 8, 8),
                (-3, -1, second[0], 3, 9), (3, 1, second[1], 4, 10), (-4, -2, second[0], 5, 5), (4, 2, second[1], 6, 6))
    TO_TARGET = ((-1, -1, whole, 0, 0), (1, 1, whole, 1, 1), (0, 0, whole, 2, 2))

    def term(away, step, rows, at, sem, flip):
        return remote(ysend.at[held(away, flip), rows], yrecv.at[at, rows], y_ss.at[sem, flip], y_rs.at[sem], ring(step, flip))

    def each_term(terms, act):
        for t in terms:
            for flip in (0, 1):
                if t[1] or flip:
                    pl.when(here(t[0]))(lambda t=t, flip=flip: act(term(*t, flip)))

    each_term(TO_RELAY, lambda copy: copy.start())

    def arrived(at, rows, sem):
        there = yrecv.at[at, rows]
        remote(there, there, y_ss.at[sem, 0], y_rs.at[sem], ring(1, 0)).wait_recv()
        return yrecv[at, rows].astype(F32)

    def relayed(way, rows, sem):
        return remote(yrelay.at[way, rows], yrecv.at[9 + way, rows], r_ss.at[way, sem], r_rs.at[way, sem], ring((-2, 2)[way], 0))

    for way in (0, 1):
        away = (-2, 2)[way]

        @pl.when(here(away))
        def _():
            yrelay[way] = ysend[held(away, 0)]

        @pl.when(jnp.logical_not(here(away)))
        def _():
            yrelay[way] = arrived(7 + way, whole, 7 + way).astype(BF16)

        there = yrelay.at[way, first[way]]
        there[...] = (there[...].astype(F32) + arrived(3 + way, first[way], 3 + way)).astype(BF16)
        relayed(way, first[way], 0).start()

    each_term(TO_TARGET, lambda copy: copy.start())

    for way in (0, 1):
        there = yrelay.at[way, second[way]]
        there[...] = (there[...].astype(F32) + arrived(3 + way, second[way], 9 + way) + arrived(5 + way, second[way], 5 + way)).astype(BF16)
        relayed(way, second[way], 1).start()

    @pl.when(at_home)
    def _():
        total[...] = ysend[held(0, 0)].astype(F32)

    @pl.when(jnp.logical_not(at_home))
    def _():
        total[...] = arrived(2, whole, 2)

    total[...] += arrived(0, whole, 0) + arrived(1, whole, 1)
    for sem, rows in ((0, first), (1, second)):
        for way in (0, 1):
            relayed(way, rows[way], sem).wait_recv()
            total[rows[way]] += yrecv[9 + way, rows[way]].astype(F32)
    out_ref[...] = total[...].astype(BF16)

    def drain(k, carry):
        for way in (0, 1):
            for h in (1, 2, 3, 4):
                hop(way, h, k).wait_send()
        pl.when(k < n - 1)(to_sibling(k).wait_send)
        for i in (1, 2, 3):
            fwd_copy(i, k).wait_send()
            bwd_copy(i, k).wait_send()
        return carry

    lax.fori_loop(0, n, drain, 0)
    for away in range(-3, 4):
        one_to_sibling(away).wait_send()
    for way in (0, 1):
        last_hop(way).wait_send()
    pl.when(jnp.logical_not(at_home))(swap_in.wait_send)
    for i, step in NEAR:
        head_near(i, step, x_ref).wait_send()
    for way in ON:
        head_on(*way).wait_send()
    each_term(TO_RELAY + TO_TARGET, lambda copy: copy.wait_send())
    for way in (0, 1):
        relayed(way, first[way], 0).wait_send()
        relayed(way, second[way], 1).wait_send()


def body(inputs, weight, grad_out):
    piece, width = inputs.shape
    part, units = weight.shape
    n = units // CHUNK
    dma = pltpu.SemaphoreType.DMA
    vmem = pl.BlockSpec(memory_space=pltpu.VMEM)
    return pl.pallas_call(
        kernel,
        out_shape=(jax.ShapeDtypeStruct((piece, units), BF16), jax.ShapeDtypeStruct((piece, width), BF16)),
        in_specs=[pl.BlockSpec(memory_space=pl.ANY)] * 3,
        out_specs=(vmem, vmem),
        scratch_shapes=[
            pltpu.VMEM((n, NZ, 2, part, CHUNK), BF16),
            pltpu.VMEM((NY, piece, width), BF16),
            pltpu.VMEM((n, NX, piece, CHUNK), BF16),
            pltpu.VMEM((n, NX - 1, piece, CHUNK), BF16),
            pltpu.VMEM((n, NX, piece, CHUNK), BF16),
            pltpu.VMEM((2, 4 * piece, width), F32),
            pltpu.VMEM((8, piece, width), BF16),
            pltpu.VMEM((11, piece, width), BF16),
            pltpu.VMEM((2, piece, width), BF16),
            pltpu.VMEM((piece, width), F32),
            pltpu.VMEM((piece, units), BF16),
            dma((2, 4, n)), dma((2, 4, n)), dma((n,)), dma((n,)), dma((n,)),
            dma((3, n)), dma((3, n)), dma((3, n)), dma((3, n)),
            dma((8,)), dma((8,)), dma((11, 2)), dma((11,)), dma((2, 2)), dma((2, 2)), dma((2,)), dma((1,)), dma, dma((9,)), dma((9,)),
        ],
        compiler_params=pltpu.CompilerParams(collective_id=0, has_side_effects=True, vmem_limit_bytes=VMEM),
        name="up_projection",
    )(inputs, weight, grad_out)


def solution(mesh):
    return jax.shard_map(
        body,
        mesh=mesh,
        in_specs=(P(("row", "dep"), "col"), P(("col", "row"), "dep"), P(("row", "col"), "dep")),
        out_specs=(P(("row", "col"), "dep"), P(("row", "dep"), "col")),
        check_vma=False,
    )
```

```python
import math

import jax
import jax.numpy as jnp
from jax import lax
from jax.experimental import pallas as pl
from jax.experimental.pallas import tpu as pltpu
from jax.sharding import PartitionSpec as P

MESH = pl.DeviceIdType.MESH
BF16, F32 = jnp.bfloat16, jnp.float32
CHUNK = 256
HOPS = (1, 3, 5, 7)
ORDER = (4, 3, 2, 1)
AHEAD = 2
NZ, NX, NY = 8, 4, 8
VMEM = 55783424
FWD, ACT, BWD = 8, 9, 11
SWAP, SPREAD = 2, 6
HELD = 1


def gelu_and_slope(v):
    c0 = math.sqrt(2.0 / math.pi)
    sq = v * v
    t = jnp.tanh(c0 * v * (1.0 + 0.044715 * sq))
    half = 0.5 * (1.0 + t)
    slope = half + 0.5 * v * (1.0 - t * t) * (c0 * (1.0 + 3.0 * 0.044715 * sq))
    return v * half, slope


def kernel(x_ref, w_ref, g_ref, hid_ref, out_ref, wbuf, xbuf, xsend, xrecv, gbuf, acc, ysend, yrecv, yrelay, total, gout,
           z_ss, z_rs, sib_ss, sib_rs, own_s, f_ss, f_rs, b_ss, b_rs, h_ss, h_rs, y_ss, y_rs, r_ss, r_rs, j_ss, j_rs, g_s, last_ss, last_rs):
    n = wbuf.shape[0]
    piece, width = xbuf.shape[1], xbuf.shape[2]
    part = w_ref.shape[0]
    cut = part // 2
    row, col, y = lax.axis_index("row"), lax.axis_index("col"), lax.axis_index("dep")
    z_hi, core = row // 2, row % 2
    z_lo, x = col // 4, col % 4
    z = 2 * z_hi + z_lo

    def dev(z_, core_, x_, y_):
        return {"row": (z_ // 2) * 2 + core_, "col": (z_ % 2) * 4 + x_, "dep": y_}

    def slot(z_):
        return (z_ % 2) * 4 + z_ // 2

    up, down = dev((z + 1) % NZ, core, x, y), dev((z + 7) % NZ, core, x, y)
    up_other, down_other = dev((z + 1) % NZ, 1 - core, x, y), dev((z + 7) % NZ, 1 - core, x, y)
    sibling = dev(z, 1 - core, x, y)
    xs = [dev(z, core, (x + i) % NX, y) for i in range(1, NX)]
    ys = {i: dev(z, core, x, (y + i + NY) % NY) for i in (1, -1, 2, -2)}
    far = {"row": row, "col": (1 - z_lo) * 4 + x, "dep": (y + 4) % NY}
    at_home = (y // 4) == z_lo

    def flipped(i):
        return {"row": row, "col": (1 - z_lo) * 4 + x, "dep": (y + i + NY) % NY}

    mine = slot(z)

    def remote(src, dst, ss, rs, to):
        return pltpu.make_async_remote_copy(src_ref=src, dst_ref=dst, send_sem=ss, recv_sem=rs, device_id=to, device_id_type=MESH)

    def cols(k):
        return pl.ds(pl.multiple_of(k * CHUNK, CHUNK), CHUNK)

    def hop(way, h, k):
        rows = pl.ds(0, part) if h < 4 else pl.ds(way * cut, cut)
        origin = (z - (h - 1) + NZ) % NZ if way == 0 else (z + (h - 1)) % NZ
        to = up if way == 0 else down
        dst = wbuf.at[k, slot(origin), core, rows]
        src = w_ref.at[:, cols(k)] if h == 1 else dst
        return remote(src, dst, z_ss.at[way, h - 1, k], z_rs.at[way, h - 1, k], to)

    def own(k):
        return pltpu.make_async_copy(w_ref.at[:, cols(k)], wbuf.at[k, mine, core], own_s.at[k])

    def to_sibling(k):
        there = wbuf.at[k, :, core]
        return remote(there, there, sib_ss.at[k], sib_rs.at[k], sibling)

    def from_sibling(k):
        there = wbuf.at[k, :, 1 - core]
        return remote(there, there, sib_ss.at[k], sib_rs.at[k], sibling)

    def one_to_sibling(away):
        there = wbuf.at[n - 1, slot((z + away + NZ) % NZ), core]
        return remote(there, there, last_ss.at[away + 3], last_rs.at[away + 3], sibling)

    def one_from_sibling(away):
        there = wbuf.at[n - 1, slot((z + away + NZ) % NZ), 1 - core]
        return remote(there, there, last_ss.at[away + 3], last_rs.at[away + 3], sibling)

    def last_hop(way):
        origin = (z + (5, 3)[way]) % NZ
        there = wbuf.at[n - 1, slot(origin), core, pl.ds(way * cut, cut)]
        return remote(there, there, last_ss.at[7 + way], last_rs.at[7 + way], (up_other, down_other)[way])

    def last_hop_arrival(way):
        there = wbuf.at[n - 1, slot((z + 4) % NZ), 1 - core, pl.ds(way * cut, cut)]
        return remote(there, there, last_ss.at[7 + way], last_rs.at[7 + way], (up_other, down_other)[way])

    x_half = piece // 2
    halves = (pl.ds(0, x_half), pl.ds(x_half, x_half))

    def fwd_copy(i, k):
        return remote(xsend.at[k, (x + i) % NX], xrecv.at[k, i - 1], f_ss.at[i - 1, k], f_rs.at[i - 1, k], xs[i - 1])

    def bwd_copy(i, k):
        return remote(gbuf.at[k, x], gbuf.at[k, x], b_ss.at[i - 1, k], b_rs.at[i - 1, k], xs[i - 1])

    def bwd_arrival(i, k):
        there = gbuf.at[k, (x + NX - i) % NX]
        return remote(there, there, b_ss.at[i - 1, k], b_rs.at[i - 1, k], xs[i - 1])

    def head_near(i, step, src):
        return remote(src, xbuf.at[y], h_ss.at[i], h_rs.at[i], ys[step])

    def head_near_arrival(i, step):
        there = xbuf.at[(y - step + NY) % NY]
        return remote(there, there, h_ss.at[i], h_rs.at[i], ys[step])

    NEAR = ((0, 2), (1, -2), (2, 1), (3, -1))

    def head_on(i, step, rows, origin):
        there = xbuf.at[(y + origin + NY) % NY, rows]
        return remote(there, there, h_ss.at[i], h_rs.at[i], ys[step])

    whole = pl.ds(0, piece)
    ON = ((4, 2, halves[0], -2), (5, -2, halves[1], 2), (6, 1, whole, -2), (7, -1, whole, 2))

    def head_on_arrival(i, step, rows, origin):
        there = xbuf.at[(y + origin - step + NY) % NY, rows]
        return remote(there, there, h_ss.at[i], h_rs.at[i], ys[step])

    barrier = pltpu.get_barrier_semaphore()
    same = [up, down, far] + xs + list(ys.values()) + [flipped(i) for i in (1, -1, 2, -2)]
    across = [sibling, up_other, down_other]
    for peer in same:
        pl.semaphore_signal(barrier, inc=1, device_id=peer, device_id_type=MESH)

    @pl.when(core == 0)
    def _():
        pl.semaphore_wait(barrier, len(same))

    @pl.when(core == 1)
    def _():
        pl.semaphore_wait(barrier, len(same) + len(across))

    for peer in across:
        pl.semaphore_signal(barrier, inc=1, device_id=peer, device_id_type=MESH)

    for k in range(AHEAD):
        hop(0, 1, k).start()
        hop(1, 1, k).start()

    swap_in = remote(x_ref, xbuf.at[(y + 4) % NY], j_ss.at[0], j_rs.at[0], far)
    swap_arrival = remote(x_ref, xbuf.at[y], j_ss.at[0], j_rs.at[0], far)
    stay_in = pltpu.make_async_copy(x_ref, xbuf.at[y], j_ss.at[1])

    @pl.when(at_home)
    def _():
        for i, step in NEAR:
            head_near(i, step, x_ref).start()
        stay_in.start()

    @pl.when(jnp.logical_not(at_home))
    def _():
        swap_in.start()

    def start_own(k, carry):
        own(k).start()
        return carry

    lax.fori_loop(0, n, start_own, 0)
    load_g = pltpu.make_async_copy(g_ref, gout, g_s)
    load_g.start()
    acc[...] = jnp.zeros_like(acc)

    def swapped():
        @pl.when(jnp.logical_not(at_home))
        def _():
            swap_arrival.wait_recv()
            for i, step in NEAR:
                head_near(i, step, xbuf.at[y]).start()

    def spread():
        for i, step in NEAR[:2]:
            head_near_arrival(i, step).wait_recv()
        for way in ON:
            head_on(*way).start()

    def within(k, f):
        pl.when(jnp.logical_and(k >= 0, k < n))(lambda: f(k))

    def pass_on(h):
        def f(k):
            for way in (0, 1):
                hop(way, h, k).wait_recv()
                if h < 4:
                    hop(way, h + 1, k).start()
                if h == 3:
                    pl.when(k == n - 1)(last_hop(way).start)
                if h < 4:
                    pl.when(k == n - 1)(one_to_sibling(h if way else -h).start)
            if h == 1:
                own(k).wait()
                pl.when(k == n - 1)(one_to_sibling(0).start)
            if h == 4:
                @pl.when(jnp.logical_and(core == 0, k == 0))
                def _():
                    pl.semaphore_wait(barrier, len(across))

                pl.when(k < n - 1)(to_sibling(k).start)
        return f

    def send_own(k):
        hop(0, 1, k).start()
        hop(1, 1, k).start()

    def forward(k):
        @pl.when(k == 0)
        def _():
            pl.when(at_home)(stay_in.wait)
            for i, step in NEAR[2:]:
                head_near_arrival(i, step).wait_recv()
            for way in ON:
                head_on_arrival(*way).wait_recv()
        pl.when(k < n - 1)(from_sibling(k).wait_recv)

        @pl.when(k == n - 1)
        def _():
            for away in range(-3, 4):
                one_from_sibling(away).wait_recv()
            for way in (0, 1):
                last_hop_arrival(way).wait_recv()

        partial = None
        for h in (0, 1):
            a = xbuf[h * 4:(h + 1) * 4].reshape(4 * piece, width)
            w = wbuf[k, h * 4:(h + 1) * 4].reshape(width, CHUNK)
            term = jnp.dot(a, w, preferred_element_type=F32)
            partial = term if partial is None else partial + term
        xsend[k] = partial.astype(BF16).reshape(NX, piece, CHUNK)

        for i in (2, 1, 3):
            fwd_copy(i, k).start()

    def activate(k):
        pl.when(k == 0)(load_g.wait)
        pre = xsend[k, x].astype(F32)
        for i in (1, 2, 3):
            fwd_copy(i, k).wait_recv()
            pre = pre + xrecv[k, i - 1].astype(F32)
        act, slope = gelu_and_slope(pre)
        gbuf[k, x] = (gout[:, cols(k)].astype(F32) * slope).astype(BF16)
        for i in (2, 1, 3):
            bwd_copy(i, k).start()
        hid_ref[:, cols(k)] = act.astype(BF16)

    def backward(k):
        for i in (1, 2, 3):
            bwd_arrival(i, k).wait_recv()
        g = gbuf[k].reshape(4 * piece, CHUNK)
        for h in (0, 1):
            w = wbuf[k, h * 4:(h + 1) * 4].reshape(width, CHUNK)
            acc[h] += lax.dot_general(g, w, (((1,), (1,)), ((), ())), preferred_element_type=F32)

    def stage(r, lag, f):
        @pl.when(r == lag + HELD)
        def _():
            lax.fori_loop(0, HELD, lambda k, carry: (f(k), carry)[1], 0)

        @pl.when(jnp.logical_and(r >= lag + HELD, r < lag + n))
        def _():
            f(r - lag)

    def one_round(r, carry):
        for h in ORDER:
            within(r - HOPS[h - 1], pass_on(h))
        within(r + AHEAD, send_own)
        pl.when(r == SWAP)(swapped)
        pl.when(r == SPREAD)(spread)
        stage(r, FWD, forward)
        stage(r, ACT, activate)
        stage(r, BWD, backward)
        return carry

    lax.fori_loop(0, n + BWD, one_round, 0)

    for h in (0, 1):
        for p in range(4):
            ysend[h * 4 + p] = acc[h, p * piece:(p + 1) * piece].astype(BF16)

    def ring(step, flip):
        return {"row": row, "col": (1 - z_lo if flip else z_lo) * 4 + x, "dep": (y + step + NY) % NY}

    def held(away, flip):
        return ((1 - z_lo if flip else z_lo) * 4 + (y + away + NY) % 4)

    def here(away):
        return ((y + away + NY) % NY) // 4 == z_lo

    first, second = (halves[1], halves[0]), (halves[0], halves[1])
    TO_RELAY = ((-3, -1, first[0], 3, 3), (3, 1, first[1], 4, 4), (-2, 0, whole, 7, 7), (2, 0, whole, 8, 8),
                (-3, -1, second[0], 3, 9), (3, 1, second[1], 4, 10), (-4, -2, second[0], 5, 5), (4, 2, second[1], 6, 6))
    OVER_Z = ((-1, 0, whole, 11, 11), (1, 0, whole, 12, 12), (0, 0, whole, 2, 2))

    def term(away, step, rows, at, sem, flip):
        return remote(ysend.at[held(away, flip), rows], yrecv.at[at, rows], y_ss.at[sem, flip], y_rs.at[sem], ring(step, flip))

    def each_term(terms, act):
        for t in terms:
            for flip in (0, 1):
                if t[1] or flip:
                    pl.when(here(t[0]))(lambda t=t, flip=flip: act(term(*t, flip)))

    each_term(TO_RELAY + OVER_Z, lambda copy: copy.start())

    def arrived(at, rows, sem):
        there = yrecv.at[at, rows]
        remote(there, there, y_ss.at[sem, 0], y_rs.at[sem], ring(1, 0)).wait_recv()
        return yrecv[at, rows].astype(F32)

    def relayed(way, rows, sem):
        return remote(yrelay.at[way, rows], yrecv.at[9 + way, rows], r_ss.at[way, sem], r_rs.at[way, sem], ring((-2, 2)[way], 0))

    for way in (0, 1):
        away = (-2, 2)[way]

        @pl.when(here(away))
        def _():
            yrelay[way] = ysend[held(away, 0)]

        @pl.when(jnp.logical_not(here(away)))
        def _():
            yrelay[way] = arrived(7 + way, whole, 7 + way).astype(BF16)

        there = yrelay.at[way, first[way]]
        there[...] = (there[...].astype(F32) + arrived(3 + way, first[way], 3 + way)).astype(BF16)
        relayed(way, first[way], 0).start()

    def to_next(way, passed):
        src = yrecv.at[11 + way] if passed else ysend.at[held((-1, 1)[way], 0)]
        return remote(src, yrecv.at[way], y_ss.at[way, 0], y_rs.at[way], ring((-1, 1)[way], 0))

    for way in (0, 1):
        pl.when(here((-1, 1)[way]))(to_next(way, False).start)

    for way in (0, 1):
        there = yrelay.at[way, second[way]]
        there[...] = (there[...].astype(F32) + arrived(3 + way, second[way], 9 + way) + arrived(5 + way, second[way], 5 + way)).astype(BF16)
        relayed(way, second[way], 1).start()

    for way in (0, 1):
        @pl.when(jnp.logical_not(here((-1, 1)[way])))
        def _():
            there = yrecv.at[11 + way]
            remote(there, there, y_ss.at[11 + way, 0], y_rs.at[11 + way], ring(1, 0)).wait_recv()
            to_next(way, True).start()

    @pl.when(at_home)
    def _():
        total[...] = ysend[held(0, 0)].astype(F32)

    @pl.when(jnp.logical_not(at_home))
    def _():
        total[...] = arrived(2, whole, 2)

    total[...] += arrived(0, whole, 0) + arrived(1, whole, 1)
    for sem, rows in ((0, first), (1, second)):
        for way in (0, 1):
            relayed(way, rows[way], sem).wait_recv()
            total[rows[way]] += yrecv[9 + way, rows[way]].astype(F32)
    out_ref[...] = total[...].astype(BF16)

    def drain(k, carry):
        for way in (0, 1):
            for h in (1, 2, 3, 4):
                hop(way, h, k).wait_send()
        pl.when(k < n - 1)(to_sibling(k).wait_send)
        for i in (1, 2, 3):
            fwd_copy(i, k).wait_send()
            bwd_copy(i, k).wait_send()
        return carry

    lax.fori_loop(0, n, drain, 0)
    for away in range(-3, 4):
        one_to_sibling(away).wait_send()
    for way in (0, 1):
        last_hop(way).wait_send()
    pl.when(jnp.logical_not(at_home))(swap_in.wait_send)
    for i, step in NEAR:
        head_near(i, step, x_ref).wait_send()
    for way in ON:
        head_on(*way).wait_send()
    each_term(TO_RELAY + OVER_Z, lambda copy: copy.wait_send())
    for way in (0, 1):
        to_next(way, True).wait_send()
    for way in (0, 1):
        relayed(way, first[way], 0).wait_send()
        relayed(way, second[way], 1).wait_send()


def body(inputs, weight, grad_out):
    piece, width = inputs.shape
    part, units = weight.shape
    n = units // CHUNK
    dma = pltpu.SemaphoreType.DMA
    vmem = pl.BlockSpec(memory_space=pltpu.VMEM)
    return pl.pallas_call(
        kernel,
        out_shape=(jax.ShapeDtypeStruct((piece, units), BF16), jax.ShapeDtypeStruct((piece, width), BF16)),
        in_specs=[pl.BlockSpec(memory_space=pl.ANY)] * 3,
        out_specs=(vmem, vmem),
        scratch_shapes=[
            pltpu.VMEM((n, NZ, 2, part, CHUNK), BF16),
            pltpu.VMEM((NY, piece, width), BF16),
            pltpu.VMEM((n, NX, piece, CHUNK), BF16),
            pltpu.VMEM((n, NX - 1, piece, CHUNK), BF16),
            pltpu.VMEM((n, NX, piece, CHUNK), BF16),
            pltpu.VMEM((2, 4 * piece, width), F32),
            pltpu.VMEM((8, piece, width), BF16),
            pltpu.VMEM((13, piece, width), BF16),
            pltpu.VMEM((2, piece, width), BF16),
            pltpu.VMEM((piece, width), F32),
            pltpu.VMEM((piece, units), BF16),
            dma((2, 4, n)), dma((2, 4, n)), dma((n,)), dma((n,)), dma((n,)),
            dma((3, n)), dma((3, n)), dma((3, n)), dma((3, n)),
            dma((8,)), dma((8,)), dma((13, 2)), dma((13,)), dma((2, 2)), dma((2, 2)), dma((2,)), dma((1,)), dma, dma((9,)), dma((9,)),
        ],
        compiler_params=pltpu.CompilerParams(collective_id=0, has_side_effects=True, vmem_limit_bytes=VMEM),
        name="up_projection",
    )(inputs, weight, grad_out)


def solution(mesh):
    return jax.shard_map(
        body,
        mesh=mesh,
        in_specs=(P(("row", "dep"), "col"), P(("col", "row"), "dep"), P(("row", "col"), "dep")),
        out_specs=(P(("row", "col"), "dep"), P(("row", "dep"), "col")),
        check_vma=False,
    )
```
